512 devices in a mesh: dp: 32 (over x, z_lo), tensor: 16 (over y, z_hi, core).
Axes of the slice: x: 4, y: 4, z: 16 (z_hi: 2, z_lo: 8; z = z_hi * 8 + z_lo), core: 2. Of those that a mesh axis runs over, the one named last changes fastest.
Arguments:
- tokens: bfloat16 [1024, 8192], P('tensor', 'dp'), may hold values from -6 to 6
- out_grad: bfloat16 [1024, 8192], P('tensor', 'dp'), may hold values from -6 to 6
- gate_pre: bfloat16 [1024, 14336], P('dp', 'tensor'), may hold values from -8 to 8
- up_pre: bfloat16 [1024, 14336], P('dp', 'tensor'), may hold values from -6 to 6
- gate_weight: bfloat16 [8192, 14336], P('dp', 'tensor'), may hold values from -0.0625 to 0.0625
- up_weight: bfloat16 [8192, 14336], P('dp', 'tensor'), may hold values from -0.0625 to 0.0625
- down_weight: bfloat16 [14336, 8192], P('tensor', 'dp'), may hold values from -0.046875 to 0.046875
Outputs:
- gate_score: float32 [8192, 14336], P('dp', 'tensor')
- up_score: float32 [8192, 14336], P('dp', 'tensor')
- down_score: float32 [14336, 8192], P('tensor', 'dp')
- input_grad: bfloat16 [1024, 8192], P('tensor', 'dp')
The draws below stay inside these ranges and needn't reach their ends.
All inputs are finite; a program needn't handle non-finite values.
Results may differ from the reference program's by a relative error of at most 0.0049.
Values may be sent and summed in bfloat16 or wider, within the bound.
No kernel may reach another device: no remote copies, remote signals or barrier semaphores. Data moves between devices by JAX's collectives and lax.ppermute only.
A program may use at most 64 MiB of HBM per device.

```python
import jax
import jax.numpy as jnp

D = 8192
FF = 14336
TOKENS = 1024


def raised(drawn, rng, source, target, blocks, factor):
    owner, partner = [(jnp.arange(drawn.shape[dim]) // (drawn.shape[dim] // blocks)).reshape([-1 if axis == dim else 1 for axis in range(drawn.ndim)]) for dim in (source, target)]
    chosen = jax.random.permutation(rng, blocks)[partner]
    strong = (owner == chosen) | (owner == (partner + blocks // 2) % blocks)
    return jnp.where(strong, factor * drawn, drawn)


def level_of(stream_key, dims, shards, smallest, top_value):
    gain = 1.0
    for dim, blocks in shards:
        steps = jax.random.uniform(jax.random.fold_in(jax.random.fold_in(stream_key, 6), dim), (blocks,), jnp.float32, smallest / len(shards), top_value / len(shards))
        gain = gain * jnp.repeat(jnp.exp(steps), dims[dim] // blocks).reshape((-1,) + (1,) * (len(dims) - 1 - dim))
    return gain


def scatter_about(key, extent, width, limit, pieces=(), kind=jnp.bfloat16):
    array = jax.random.normal(key, extent, jnp.float32) * width
    if len(pieces) > 0:
        array = level_of(key, extent, pieces, -0.22, 0.18) * array
    return jnp.clip(array, min=-limit, max=limit).astype(kind)


def heavy_noise(stream_key, dims, spread, reach, cuts, heavy, dtype=jnp.bfloat16):
    entries = spread * jax.random.normal(stream_key, dims, jnp.float32)
    if cuts:
        entries = entries * level_of(stream_key, dims, cuts, -0.22, 0.18)
    return jnp.clip(raised(entries, jax.random.fold_in(stream_key, 3), *heavy), -reach, reach).astype(dtype)


def setup_inputs(seed: int = 0) -> dict:
    keys = jax.random.split(jax.random.key(seed), 8)
    return {
        "tokens": scatter_about(keys[0], (TOKENS, D), 1.0, 6.0, ((0, 16), (1, 32))),
        "out_grad": heavy_noise(keys[1], (TOKENS, D), 1.0, 6.0, ((0, 16), (1, 32)), (1, 0, 32, 2.75)),
        "gate_pre": scatter_about(keys[2], (TOKENS, FF), 1.5, 8.0, ((0, 32), (1, 16))),
        "up_pre": scatter_about(keys[3], (TOKENS, FF), 1.0, 6.0, ((0, 32), (1, 16))),
        "gate_weight": scatter_about(keys[4], (D, FF), D ** -0.5, 0.0625, ((0, 32), (1, 16))),
        "up_weight": scatter_about(keys[5], (D, FF), D ** -0.5, 0.0625, ((0, 32), (1, 16))),
        "down_weight": scatter_about(keys[6], (FF, D), FF ** -0.5, 0.046875, ((0, 16), (1, 32))),
    }


def reference(tokens, out_grad, gate_pre, up_pre, gate_weight, up_weight, down_weight):
    gate_float = gate_pre.astype(jnp.float32)
    up_float = up_pre.astype(jnp.float32)
    gate_sigmoid = 1.0 / (1.0 + jnp.exp(-gate_float))
    active = (gate_float * gate_sigmoid * up_float).astype(jnp.bfloat16)
    down_sum = jnp.dot(active.T, out_grad, preferred_element_type=jnp.float32)
    hidden_grad = jnp.dot(out_grad, down_weight.T, preferred_element_type=jnp.float32)
    gate_grad = (hidden_grad * up_float * gate_sigmoid * (1.0 + gate_float * (1.0 - gate_sigmoid))).astype(jnp.bfloat16)
    up_grad = (hidden_grad * gate_float * gate_sigmoid).astype(jnp.bfloat16)
    gate_sum = jnp.dot(tokens.T, gate_grad, preferred_element_type=jnp.float32)
    up_sum = jnp.dot(tokens.T, up_grad, preferred_element_type=jnp.float32)
    input_grad = (jnp.dot(gate_grad, gate_weight.T, preferred_element_type=jnp.float32)
                  + jnp.dot(up_grad, up_weight.T, preferred_element_type=jnp.float32)).astype(jnp.bfloat16)
    gate_score = jnp.abs(gate_weight.astype(jnp.float32) * gate_sum)
    up_score = jnp.abs(up_weight.astype(jnp.float32) * up_sum)
    down_score = jnp.abs(down_weight.astype(jnp.float32) * down_sum)
    return (gate_score, up_score, down_score, input_grad)
```

```python
import jax
import jax.numpy as jnp
from jax import lax
from jax.sharding import PartitionSpec as P

X, ZL, Y, ZH, C = 4, 8, 4, 2, 2
X_GROUPS = [[x * ZL + z for x in range(X)] for z in range(ZL)]
Z_GROUPS = [[x * ZL + z for z in range(ZL)] for x in range(X)]
ZH_GROUPS = [[(y * ZH + h) * C + c for h in range(ZH)] for y in range(Y) for c in range(C)]
Y_GROUPS = [[(y * ZH + h) * C + c for y in range(Y)] for h in range(ZH) for c in range(C)]
C_GROUPS = [[(y * ZH + h) * C + c for c in range(C)] for y in range(Y) for h in range(ZH)]
YZH_GROUPS = [[(y * ZH + h) * C + c for y in range(Y) for h in range(ZH)] for c in range(C)]


def exchange(blocks, axis, groups):
    return lax.all_to_all(blocks, axis, 0, 0, axis_index_groups=groups, tiled=True)


def gather(block, axis, groups):
    copies = jnp.broadcast_to(block[None], (len(groups[0]),) + block.shape)
    return exchange(copies, axis, groups)


def add_up(blocks, axis, groups):
    return jnp.sum(exchange(blocks, axis, groups).astype(jnp.float32), axis=0)


def on_device(tokens, out_grad, gate_pre, up_pre, gate_weight, up_weight, down_weight):
    rows, feats = out_grad.shape
    toks, hid = gate_pre.shape
    n = rows * Y * ZH * C

    both = jnp.stack([out_grad, tokens])
    both = gather(both, "tensor", ZH_GROUPS)
    both = gather(both, "tensor", Y_GROUPS)
    both = gather(both, "tensor", C_GROUPS)
    both = both.transpose(3, 1, 2, 0, 4, 5).reshape(2, n, feats)
    grads_all, tokens_all = both[0], both[1]

    saved = jnp.stack([gate_pre, up_pre])
    saved = gather(saved, "dp", Z_GROUPS)
    saved = gather(saved, "dp", X_GROUPS)
    gate_all = saved[:, :, 0].reshape(n, hid)
    up_all = saved[:, :, 1].reshape(n, hid)

    partial = jnp.einsum(
        "nd,fd->nf", grads_all, down_weight, preferred_element_type=jnp.float32
    ).astype(jnp.bfloat16)
    hidden = add_up(partial.reshape(X, ZL * toks, hid), "dp", X_GROUPS).astype(jnp.bfloat16)
    hidden = add_up(hidden.reshape(ZL, toks, hid), "dp", Z_GROUPS).astype(jnp.bfloat16)
    hidden = gather(hidden, "dp", Z_GROUPS)
    hidden = gather(hidden, "dp", X_GROUPS).reshape(n, hid).astype(jnp.float32)

    gate_float = gate_all.astype(jnp.float32)
    up_float = up_all.astype(jnp.float32)
    gate_sigmoid = 1.0 / (1.0 + jnp.exp(-gate_float))
    active = (gate_float * gate_sigmoid * up_float).astype(jnp.bfloat16)
    gate_grad = (
        hidden * up_float * gate_sigmoid * (1.0 + gate_float * (1.0 - gate_sigmoid))
    ).astype(jnp.bfloat16)
    up_grad = (hidden * gate_float * gate_sigmoid).astype(jnp.bfloat16)

    partial_in = jnp.einsum(
        "nf,df->nd", gate_grad, gate_weight, preferred_element_type=jnp.float32
    ) + jnp.einsum("nf,df->nd", up_grad, up_weight, preferred_element_type=jnp.float32)
    partial_in = partial_in.reshape(Y * ZH, C, rows, feats).transpose(1, 0, 2, 3)
    partial_in = add_up(partial_in, "tensor", C_GROUPS).astype(jnp.bfloat16)
    input_grad = add_up(partial_in, "tensor", YZH_GROUPS).astype(jnp.bfloat16)

    down_sum = jnp.einsum("nf,nd->fd", active, grads_all, preferred_element_type=jnp.float32)
    gate_sum = jnp.einsum("nd,nf->df", tokens_all, gate_grad, preferred_element_type=jnp.float32)
    up_sum = jnp.einsum("nd,nf->df", tokens_all, up_grad, preferred_element_type=jnp.float32)
    gate_score = jnp.abs(gate_weight.astype(jnp.float32) * gate_sum)
    up_score = jnp.abs(up_weight.astype(jnp.float32) * up_sum)
    down_score = jnp.abs(down_weight.astype(jnp.float32) * down_sum)
    return (gate_score, up_score, down_score, input_grad)


def solution(mesh):
    return jax.shard_map(
        on_device,
        mesh=mesh,
        in_specs=(
            P("tensor", "dp"),
            P("tensor", "dp"),
            P("dp", "tensor"),
            P("dp", "tensor"),
            P("dp", "tensor"),
            P("dp", "tensor"),
            P("tensor", "dp"),
        ),
        out_specs=(P("dp", "tensor"), P("dp", "tensor"), P("tensor", "dp"), P("tensor", "dp")),
        check_vma=False,
    )
```

```python
import jax
import jax.numpy as jnp
from jax import lax
from jax.sharding import PartitionSpec as P

X, ZL, Y, ZH, C = 4, 8, 4, 2, 2
X_GROUPS = [[x * ZL + z for x in range(X)] for z in range(ZL)]
Z_GROUPS = [[x * ZL + z for z in range(ZL)] for x in range(X)]
Y_GROUPS = [[(y * ZH + h) * C + c for y in range(Y)] for h in range(ZH) for c in range(C)]
C_GROUPS = [[(y * ZH + h) * C + c for c in range(C)] for y in range(Y) for h in range(ZH)]
YZH_GROUPS = [[(y * ZH + h) * C + c for y in range(Y) for h in range(ZH)] for c in range(C)]
ZH_SWAP = [(t, t ^ C) for t in range(Y * ZH * C)]
C_SWAP = [(t, t ^ 1) for t in range(Y * ZH * C)]
X_UP = [(x * ZL + z, (x + 1) % X * ZL + z) for x in range(X) for z in range(ZL)]
X_DOWN = [(x * ZL + z, (x - 1) % X * ZL + z) for x in range(X) for z in range(ZL)]


def exchange(blocks, axis, groups):
    return lax.all_to_all(blocks, axis, 0, 0, axis_index_groups=groups, tiled=True)


def gather(block, axis, groups):
    copies = jnp.broadcast_to(block[None], (len(groups[0]),) + block.shape)
    return exchange(copies, axis, groups)


def add_up(blocks, axis, groups):
    return jnp.sum(exchange(blocks, axis, groups).astype(jnp.float32), axis=0)


def pair(block, axis, perm, bit, dim):
    other = lax.ppermute(block, axis, perm)
    first = jnp.where(bit == 0, block, other)
    second = jnp.where(bit == 0, other, block)
    return jnp.stack([first, second], axis=dim)


def on_device(tokens, out_grad, gate_pre, up_pre, gate_weight, up_weight, down_weight):
    rows, feats = out_grad.shape
    toks, hid = gate_pre.shape
    n = rows * Y * ZH * C
    dp, tensor = lax.axis_index("dp"), lax.axis_index("tensor")
    x, z = dp // ZL, dp % ZL

    both = jnp.stack([out_grad, tokens])
    both = pair(both, "tensor", ZH_SWAP, tensor // C % ZH, 0)

    down_all = gather(down_weight, "dp", X_GROUPS)

    both = lax.all_gather(both, "tensor", axis_index_groups=Y_GROUPS)
    both = both.transpose(2, 0, 1, 3, 4).reshape(2, Y * ZH, rows, feats)
    both = pair(both, "tensor", C_SWAP, tensor % C, 2)
    both = both.reshape(2, n, feats)
    grads_all, tokens_all = both[0], both[1]

    saved = jnp.stack([gate_pre, up_pre])
    for dim, reach in enumerate((4, 2, 1)):
        swap = [(d, d ^ reach) for d in range(X * ZL)]
        saved = pair(saved, "dp", swap, z // reach % 2, dim)
    saved = saved.reshape(ZL, 2, toks, hid)

    ahead, down_all, saved = lax.optimization_barrier((grads_all, down_all, saved))
    grads_x = exchange(ahead.reshape(X, n // X, feats), "dp", X_GROUPS)
    partial = sum(
        jnp.einsum("nd,fd->nf", grads_x[k], down_all[k], preferred_element_type=jnp.float32)
        for k in range(X)
    ).astype(jnp.bfloat16)

    from_down = lax.ppermute(saved, "dp", X_UP)
    from_up = lax.ppermute(saved, "dp", X_DOWN)

    hidden = add_up(partial.reshape(ZL, toks, hid), "dp", Z_GROUPS).astype(jnp.bfloat16)

    far_low = lax.ppermute(from_down[: ZL // 2], "dp", X_UP)
    far_high = lax.ppermute(from_up[ZL // 2 :], "dp", X_DOWN)

    hidden = gather(hidden, "dp", Z_GROUPS)
    hidden = gather(hidden, "dp", X_GROUPS).reshape(n, hid).astype(jnp.float32)

    full = jnp.zeros((X,) + saved.shape, saved.dtype)
    for block, start, half in (
        (saved, x, 0),
        (from_down, (x + X - 1) % X, 0),
        (from_up, (x + 1) % X, 0),
        (far_low, (x + 2) % X, 0),
        (far_high, (x + 2) % X, ZL // 2),
    ):
        full = lax.dynamic_update_slice(full, block[None], (start, half, 0, 0, 0))
    gate_all = full[:, :, 0].reshape(n, hid)
    up_all = full[:, :, 1].reshape(n, hid)

    gate_float = gate_all.astype(jnp.float32)
    up_float = up_all.astype(jnp.float32)
    gate_sigmoid = 1.0 / (1.0 + jnp.exp(-gate_float))
    active = (gate_float * gate_sigmoid * up_float).astype(jnp.bfloat16)
    gate_grad = (
        hidden * up_float * gate_sigmoid * (1.0 + gate_float * (1.0 - gate_sigmoid))
    ).astype(jnp.bfloat16)
    up_grad = (hidden * gate_float * gate_sigmoid).astype(jnp.bfloat16)

    partial_in = jnp.einsum(
        "nf,df->nd", gate_grad, gate_weight, preferred_element_type=jnp.float32
    ) + jnp.einsum("nf,df->nd", up_grad, up_weight, preferred_element_type=jnp.float32)
    partial_in = partial_in.reshape(Y * ZH, C, rows, feats).transpose(1, 0, 2, 3)
    partial_in = add_up(partial_in, "tensor", C_GROUPS).astype(jnp.bfloat16)
    input_grad = add_up(partial_in, "tensor", YZH_GROUPS).astype(jnp.bfloat16)

    down_sum = jnp.einsum("nf,nd->fd", active, grads_all, preferred_element_type=jnp.float32)
    gate_sum = jnp.einsum("nd,nf->df", tokens_all, gate_grad, preferred_element_type=jnp.float32)
    up_sum = jnp.einsum("nd,nf->df", tokens_all, up_grad, preferred_element_type=jnp.float32)
    gate_score = jnp.abs(gate_weight.astype(jnp.float32) * gate_sum)
    up_score = jnp.abs(up_weight.astype(jnp.float32) * up_sum)
    down_score = jnp.abs(down_weight.astype(jnp.float32) * down_sum)
    return (gate_score, up_score, down_score, input_grad)


def solution(mesh):
    return jax.shard_map(
        on_device,
        mesh=mesh,
        in_specs=(
            P("tensor", "dp"),
            P("tensor", "dp"),
            P("dp", "tensor"),
            P("dp", "tensor"),
            P("dp", "tensor"),
            P("dp", "tensor"),
            P("tensor", "dp"),
        ),
        out_specs=(P("dp", "tensor"), P("dp", "tensor"), P("tensor", "dp"), P("tensor", "dp")),
        check_vma=False,
    )
```

```python
import jax
import jax.numpy as jnp
from jax import lax
from jax.sharding import PartitionSpec as P

X, ZL, Y, ZH, C = 4, 8, 4, 2, 2
X_GROUPS = [[x * ZL + z for x in range(X)] for z in range(ZL)]
Z_GROUPS = [[x * ZL + z for z in range(ZL)] for x in range(X)]
Z_BY_CORE = [
    [x * ZL + (h * C + c) * 2 + k for c in range(C) for h in range(ZH) for k in range(2)]
    for x in range(X)
]
Y_GROUPS = [[(y * ZH + h) * C + c for y in range(Y)] for h in range(ZH) for c in range(C)]
C_GROUPS = [[(y * ZH + h) * C + c for c in range(C)] for y in range(Y) for h in range(ZH)]
ZH_SWAP = [(t, t ^ C) for t in range(Y * ZH * C)]
C_SWAP = [(t, t ^ 1) for t in range(Y * ZH * C)]
X_UP = [(x * ZL + z, (x + 1) % X * ZL + z) for x in range(X) for z in range(ZL)]
X_DOWN = [(x * ZL + z, (x - 1) % X * ZL + z) for x in range(X) for z in range(ZL)]


def exchange(blocks, axis, groups):
    return lax.all_to_all(blocks, axis, 0, 0, axis_index_groups=groups, tiled=True)


def gather(block, axis, groups):
    copies = jnp.broadcast_to(block[None], (len(groups[0]),) + block.shape)
    return exchange(copies, axis, groups)


def add_up(blocks, axis, groups):
    return jnp.sum(exchange(blocks, axis, groups).astype(jnp.float32), axis=0)


def pair(block, axis, perm, bit, dim):
    other = lax.ppermute(block, axis, perm)
    first = jnp.where(bit == 0, block, other)
    second = jnp.where(bit == 0, other, block)
    return jnp.stack([first, second], axis=dim)


def on_device(tokens, out_grad, gate_pre, up_pre, gate_weight, up_weight, down_weight):
    rows, feats = out_grad.shape
    toks, hid = gate_pre.shape
    n = rows * Y * ZH * C
    dp, tensor = lax.axis_index("dp"), lax.axis_index("tensor")
    x, z = dp // ZL, dp % ZL

    both = jnp.stack([out_grad, tokens])
    both = pair(both, "tensor", ZH_SWAP, tensor // C % ZH, 1)
    grads_y = lax.all_gather(both[0], "tensor", axis_index_groups=Y_GROUPS)

    down_all = gather(down_weight, "dp", X_GROUPS)

    saved = jnp.stack([gate_pre, up_pre])
    for dim, reach in enumerate((4, 2, 1)):
        swap = [(d, d ^ reach) for d in range(X * ZL)]
        if reach == 2:
            saved, grads_y = lax.optimization_barrier((saved, grads_y))
        if reach == 1:
            saved, down_all, ahead = lax.optimization_barrier((saved, down_all, grads_y))
        saved = pair(saved, "dp", swap, z // reach % 2, dim)
    saved = saved.reshape(ZL, 2, toks, hid)

    grads_x = exchange(ahead, "dp", X_GROUPS)
    grads_x = lax.all_gather(grads_x, "tensor", axis_index_groups=C_GROUPS)
    grads_x, saved = lax.optimization_barrier((grads_x, saved))
    partial = sum(
        jnp.einsum(
            "nd,fd->nf",
            grads_x[:, k].reshape(n // X, feats),
            down_all[k],
            preferred_element_type=jnp.float32,
        )
        for k in range(X)
    ).astype(jnp.bfloat16)

    inputs, _ = lax.optimization_barrier((both[1], partial))
    tokens_y = lax.all_gather(inputs, "tensor", axis_index_groups=Y_GROUPS)
    both = jnp.stack([grads_y, tokens_y]).reshape(2, Y * ZH, rows, feats)
    both = pair(both, "tensor", C_SWAP, tensor % C, 2)
    both = both.reshape(2, n, feats)
    grads_all, tokens_all = both[0], both[1]

    from_down = lax.ppermute(saved, "dp", X_UP)
    from_up = lax.ppermute(saved, "dp", X_DOWN)

    hidden = add_up(partial.reshape(ZL, toks, hid), "dp", Z_BY_CORE).astype(jnp.bfloat16)

    far_low = lax.ppermute(from_down[: ZL // 2], "dp", X_UP)
    far_high = lax.ppermute(from_up[ZL // 2 :], "dp", X_DOWN)

    hidden = gather(hidden, "dp", Z_GROUPS)
    hidden = gather(hidden, "dp", X_GROUPS).reshape(n, hid).astype(jnp.float32)

    full = jnp.zeros((X,) + saved.shape, saved.dtype)
    for block, start, half in (
        (saved, x, 0),
        (from_down, (x + X - 1) % X, 0),
        (from_up, (x + 1) % X, 0),
        (far_low, (x + 2) % X, 0),
        (far_high, (x + 2) % X, ZL // 2),
    ):
        full = lax.dynamic_update_slice(full, block[None], (start, half, 0, 0, 0))
    gate_all = full[:, :, 0].reshape(n, hid)
    up_all = full[:, :, 1].reshape(n, hid)

    gate_float = gate_all.astype(jnp.float32)
    up_float = up_all.astype(jnp.float32)
    gate_sigmoid = 1.0 / (1.0 + jnp.exp(-gate_float))
    active = (gate_float * gate_sigmoid * up_float).astype(jnp.bfloat16)
    gate_grad = (
        hidden * up_float * gate_sigmoid * (1.0 + gate_float * (1.0 - gate_sigmoid))
    ).astype(jnp.bfloat16)
    up_grad = (hidden * gate_float * gate_sigmoid).astype(jnp.bfloat16)

    partial_in = jnp.einsum(
        "nf,df->nd", gate_grad, gate_weight, preferred_element_type=jnp.float32
    ) + jnp.einsum("nf,df->nd", up_grad, up_weight, preferred_element_type=jnp.float32)
    partial_in = partial_in.reshape(Y * ZH, C, rows, feats).transpose(1, 0, 2, 3)
    partial_in = add_up(partial_in, "tensor", C_GROUPS).astype(jnp.bfloat16)
    partial_in = add_up(partial_in.reshape(Y, ZH, rows, feats), "tensor", Y_GROUPS)
    upper = tensor // C % ZH == 1
    sent = jnp.where(upper, partial_in[0], partial_in[1])
    kept = jnp.where(upper, partial_in[1], partial_in[0])
    input_grad = (kept + lax.ppermute(sent, "tensor", ZH_SWAP)).astype(jnp.bfloat16)

    down_sum = jnp.einsum("nf,nd->fd", active, grads_all, preferred_element_type=jnp.float32)
    gate_sum = jnp.einsum("nd,nf->df", tokens_all, gate_grad, preferred_element_type=jnp.float32)
    up_sum = jnp.einsum("nd,nf->df", tokens_all, up_grad, preferred_element_type=jnp.float32)
    gate_score = jnp.abs(gate_weight.astype(jnp.float32) * gate_sum)
    up_score = jnp.abs(up_weight.astype(jnp.float32) * up_sum)
    down_score = jnp.abs(down_weight.astype(jnp.float32) * down_sum)
    return (gate_score, up_score, down_score, input_grad)


def solution(mesh):
    return jax.shard_map(
        on_device,
        mesh=mesh,
        in_specs=(
            P("tensor", "dp"),
            P("tensor", "dp"),
            P("dp", "tensor"),
            P("dp", "tensor"),
            P("dp", "tensor"),
            P("dp", "tensor"),
            P("tensor", "dp"),
        ),
        out_specs=(P("dp", "tensor"), P("dp", "tensor"), P("tensor", "dp"), P("tensor", "dp")),
        check_vma=False,
    )
```

```python
import jax
import jax.numpy as jnp
from jax import lax
from jax.sharding import PartitionSpec as P

X, ZL, Y, ZH, C = 4, 8, 4, 2, 2
X_GROUPS = [[x * ZL + z for x in range(X)] for z in range(ZL)]
Z_GROUPS = [[x * ZL + z for z in range(ZL)] for x in range(X)]
Z_BY_CORE = [
    [x * ZL + (h * C + c) * 2 + k for c in range(C) for h in range(ZH) for k in range(2)]
    for x in range(X)
]
YC_GROUPS = [[(y * ZH + h) * C + c for y in range(Y) for c in range(C)] for h in range(ZH)]
Y_GROUPS = [[(y * ZH + h) * C + c for y in range(Y)] for h in range(ZH) for c in range(C)]
C_GROUPS = [[(y * ZH + h) * C + c for c in range(C)] for y in range(Y) for h in range(ZH)]
ZH_SWAP = [(t, t ^ C) for t in range(Y * ZH * C)]
C_SWAP = [(t, t ^ 1) for t in range(Y * ZH * C)]
X_UP = [(x * ZL + z, (x + 1) % X * ZL + z) for x in range(X) for z in range(ZL)]
X_DOWN = [(x * ZL + z, (x - 1) % X * ZL + z) for x in range(X) for z in range(ZL)]


def exchange(blocks, axis, groups):
    return lax.all_to_all(blocks, axis, 0, 0, axis_index_groups=groups, tiled=True)


def gather(block, axis, groups):
    copies = jnp.broadcast_to(block[None], (len(groups[0]),) + block.shape)
    return exchange(copies, axis, groups)


def add_up(blocks, axis, groups):
    return jnp.sum(exchange(blocks, axis, groups).astype(jnp.float32), axis=0)


def pair(block, axis, perm, bit, dim):
    other = lax.ppermute(block, axis, perm)
    first = jnp.where(bit == 0, block, other)
    second = jnp.where(bit == 0, other, block)
    return jnp.stack([first, second], axis=dim)


def around(block, held):
    half = block.shape[0] // 2
    before = lax.ppermute(block, "dp", X_UP)
    after = lax.ppermute(block, "dp", X_DOWN)
    before, after, held = lax.optimization_barrier((before, after, held))
    far_low = lax.ppermute(before[:half], "dp", X_UP)
    far_high = lax.ppermute(after[half:], "dp", X_DOWN)
    return [block, after, jnp.concatenate([far_low, far_high]), before], held


def on_device(tokens, out_grad, gate_pre, up_pre, gate_weight, up_weight, down_weight):
    rows, feats = out_grad.shape
    toks, hid = gate_pre.shape
    part = rows * ZH * C
    dp, tensor = lax.axis_index("dp"), lax.axis_index("tensor")
    x, z = dp // ZL, dp % ZL

    both = jnp.stack([out_grad, tokens])
    both = pair(both, "tensor", ZH_SWAP, tensor // C % ZH, 1)

    down_ring, both = around(down_weight, both)
    grads_y = gather(both[0], "tensor", Y_GROUPS)

    saved = jnp.stack([gate_pre, up_pre])
    for dim, reach in enumerate((4, 2)):
        swap = [(d, d ^ reach) for d in range(X * ZL)]
        if reach == 2:
            saved, grads_y = lax.optimization_barrier((saved, grads_y))
        saved = pair(saved, "dp", swap, z // reach % 2, dim)

    grads_x = exchange(grads_y, "dp", X_GROUPS)
    grads_x = lax.all_gather(grads_x, "tensor", axis_index_groups=C_GROUPS)
    grads_x, saved = lax.optimization_barrier((grads_x, saved))
    partial = sum(
        jnp.einsum(
            "nd,fd->nf",
            lax.dynamic_index_in_dim(grads_x, (x + k) % X, 1, False).reshape(part, feats),
            down_ring[k],
            preferred_element_type=jnp.float32,
        )
        for k in range(X)
    ).astype(jnp.bfloat16)

    saved = pair(saved, "dp", [(d, d ^ 1) for d in range(X * ZL)], z % 2, 2)
    saved_ring, _ = around(saved.reshape(ZL, 2, toks, hid), ())

    inputs, _ = lax.optimization_barrier((both[1], partial))
    tokens_y = lax.all_gather(inputs, "tensor", axis_index_groups=Y_GROUPS)
    both = jnp.stack([grads_y, tokens_y])
    both = lax.dynamic_slice_in_dim(jnp.concatenate([both, both], axis=1), x, Y, 1)
    both = pair(both, "tensor", C_SWAP, tensor % C, 3)
    both = both.reshape(2, Y, part, feats)
    grads_ring, tokens_ring = both[0], both[1]

    hidden = add_up(partial.reshape(ZL, toks, hid), "dp", Z_BY_CORE).astype(jnp.bfloat16)
    hidden = gather(hidden, "dp", Z_GROUPS)
    hidden_ring, own = around(hidden, hidden)
    hidden_ring[0] = own

    down_sum = gate_sum = up_sum = 0.0
    partial_in = jnp.zeros((Y, C, ZH, rows, feats), jnp.bfloat16)
    for k in (0, 1, 3, 2):
        gate_float = saved_ring[k][:, 0].reshape(part, hid).astype(jnp.float32)
        up_float = saved_ring[k][:, 1].reshape(part, hid).astype(jnp.float32)
        hidden = hidden_ring[k].reshape(part, hid).astype(jnp.float32)
        gate_sigmoid = 1.0 / (1.0 + jnp.exp(-gate_float))
        active = (gate_float * gate_sigmoid * up_float).astype(jnp.bfloat16)
        gate_grad = (
            hidden * up_float * gate_sigmoid * (1.0 + gate_float * (1.0 - gate_sigmoid))
        ).astype(jnp.bfloat16)
        up_grad = (hidden * gate_float * gate_sigmoid).astype(jnp.bfloat16)
        gate_grad, up_grad = lax.optimization_barrier((gate_grad, up_grad))
        block = jnp.einsum(
            "nf,df->nd", gate_grad, gate_weight, preferred_element_type=jnp.float32
        ) + jnp.einsum("nf,df->nd", up_grad, up_weight, preferred_element_type=jnp.float32)
        block = block.astype(jnp.bfloat16).reshape(1, ZH, C, rows, feats).swapaxes(1, 2)
        partial_in = lax.dynamic_update_slice_in_dim(partial_in, block, (x + k) % X, 0)
        down_sum += jnp.einsum(
            "nf,nd->fd", active, grads_ring[k], preferred_element_type=jnp.float32
        )
        gate_sum += jnp.einsum(
            "nd,nf->df", tokens_ring[k], gate_grad, preferred_element_type=jnp.float32
        )
        up_sum += jnp.einsum(
            "nd,nf->df", tokens_ring[k], up_grad, preferred_element_type=jnp.float32
        )

    partial_in = partial_in.reshape(Y * C, ZH, rows, feats)
    partial_in = add_up(partial_in, "tensor", YC_GROUPS)
    upper = tensor // C % ZH == 1
    sent = jnp.where(upper, partial_in[0], partial_in[1])
    kept = jnp.where(upper, partial_in[1], partial_in[0])
    input_grad = (kept + lax.ppermute(sent, "tensor", ZH_SWAP)).astype(jnp.bfloat16)

    gate_score = jnp.abs(gate_weight.astype(jnp.float32) * gate_sum)
    up_score = jnp.abs(up_weight.astype(jnp.float32) * up_sum)
    down_score = jnp.abs(down_weight.astype(jnp.float32) * down_sum)
    return (gate_score, up_score, down_score, input_grad)


def solution(mesh):
    return jax.shard_map(
        on_device,
        mesh=mesh,
        in_specs=(
            P("tensor", "dp"),
            P("tensor", "dp"),
            P("dp", "tensor"),
            P("dp", "tensor"),
            P("dp", "tensor"),
            P("dp", "tensor"),
            P("tensor", "dp"),
        ),
        out_specs=(P("dp", "tensor"), P("dp", "tensor"), P("tensor", "dp"), P("tensor", "dp")),
        check_vma=False,
    )
```

```python
import jax
import jax.numpy as jnp
from jax import lax
from jax.sharding import PartitionSpec as P

X, ZL, Y, ZH, C = 4, 8, 4, 2, 2
X_GROUPS = [[x * ZL + z for x in range(X)] for z in range(ZL)]
Z_GROUPS = [[x * ZL + z for z in range(ZL)] for x in range(X)]
Z_BY_CORE = [
    [x * ZL + (h * C + c) * 2 + k for c in range(C) for h in range(ZH) for k in range(2)]
    for x in range(X)
]
YC_GROUPS = [[(y * ZH + h) * C + c for y in range(Y) for c in range(C)] for h in range(ZH)]
Y_GROUPS = [[(y * ZH + h) * C + c for y in range(Y)] for h in range(ZH) for c in range(C)]
C_GROUPS = [[(y * ZH + h) * C + c for c in range(C)] for y in range(Y) for h in range(ZH)]
ZH_SWAP = [(t, t ^ C) for t in range(Y * ZH * C)]
C_SWAP = [(t, t ^ 1) for t in range(Y * ZH * C)]
X_UP = [(x * ZL + z, (x + 1) % X * ZL + z) for x in range(X) for z in range(ZL)]
X_DOWN = [(x * ZL + z, (x - 1) % X * ZL + z) for x in range(X) for z in range(ZL)]


def exchange(blocks, axis, groups):
    return lax.all_to_all(blocks, axis, 0, 0, axis_index_groups=groups, tiled=True)


def gather(block, axis, groups):
    copies = jnp.broadcast_to(block[None], (len(groups[0]),) + block.shape)
    return exchange(copies, axis, groups)


def add_up(blocks, axis, groups):
    return jnp.sum(exchange(blocks, axis, groups).astype(jnp.float32), axis=0)


def pair(block, axis, perm, bit, dim):
    other = lax.ppermute(block, axis, perm)
    first = jnp.where(bit == 0, block, other)
    second = jnp.where(bit == 0, other, block)
    return jnp.stack([first, second], axis=dim)


def on_device(tokens, out_grad, gate_pre, up_pre, gate_weight, up_weight, down_weight):
    rows, feats = out_grad.shape
    toks, hid = gate_pre.shape
    n = rows * Y * ZH * C
    dp, tensor = lax.axis_index("dp"), lax.axis_index("tensor")
    x, z = dp // ZL, dp % ZL

    copies = jnp.broadcast_to(down_weight[None], (X,) + down_weight.shape)
    copies, out_grad, tokens, gate_pre, up_pre = lax.optimization_barrier(
        (copies, out_grad, tokens, gate_pre, up_pre)
    )
    down_all = exchange(copies, "dp", X_GROUPS)

    both = jnp.stack([out_grad, tokens])
    both = pair(both, "tensor", ZH_SWAP, tensor // C % ZH, 1)
    grads_y = lax.all_gather(both[0], "tensor", axis_index_groups=Y_GROUPS)

    saved = jnp.stack([gate_pre, up_pre])
    saved = pair(saved, "dp", [(d, d ^ 4) for d in range(X * ZL)], z // 4, 0)
    saved, grads_y = lax.optimization_barrier((saved, grads_y))
    saved = pair(saved, "dp", [(d, d ^ 2) for d in range(X * ZL)], z // 2 % 2, 1)

    down_all, ahead = lax.optimization_barrier((down_all, grads_y))
    grads_x = exchange(ahead, "dp", X_GROUPS)
    grads_x = lax.all_gather(grads_x, "tensor", axis_index_groups=C_GROUPS)
    grads_x, saved = lax.optimization_barrier((grads_x, saved))
    saved = pair(saved, "dp", [(d, d ^ 1) for d in range(X * ZL)], z % 2, 2)
    saved = saved.reshape(ZL, 2, toks, hid)
    partial = sum(
        jnp.einsum(
            "nd,fd->nf",
            grads_x[:, k].reshape(n // X, feats),
            down_all[k],
            preferred_element_type=jnp.float32,
        )
        for k in range(X)
    ).astype(jnp.bfloat16)

    inputs, _ = lax.optimization_barrier((both[1], partial))
    tokens_y = lax.all_gather(inputs, "tensor", axis_index_groups=Y_GROUPS)
    both = jnp.stack([grads_y, tokens_y]).reshape(2, Y * ZH, rows, feats)
    both = pair(both, "tensor", C_SWAP, tensor % C, 2)
    both = both.reshape(2, n, feats)
    grads_all, tokens_all = both[0], both[1]

    from_down = lax.ppermute(saved, "dp", X_UP)
    from_up = lax.ppermute(saved, "dp", X_DOWN)

    hidden = add_up(partial.reshape(ZL, toks, hid), "dp", Z_BY_CORE).astype(jnp.bfloat16)

    far_low = lax.ppermute(from_down[: ZL // 2], "dp", X_UP)
    far_high = lax.ppermute(from_up[ZL // 2 :], "dp", X_DOWN)

    hidden = gather(hidden, "dp", Z_GROUPS)
    hidden = gather(hidden, "dp", X_GROUPS).reshape(n, hid).astype(jnp.float32)

    full = jnp.broadcast_to(saved[None], (X,) + saved.shape)
    for block, start, half in (
        (from_down, (x + X - 1) % X, 0),
        (from_up, (x + 1) % X, 0),
        (far_low, (x + 2) % X, 0),
        (far_high, (x + 2) % X, ZL // 2),
    ):
        full = lax.dynamic_update_slice(full, block[None], (start, half, 0, 0, 0))
    gate_all = full[:, :, 0].reshape(n, hid)
    up_all = full[:, :, 1].reshape(n, hid)

    gate_float = gate_all.astype(jnp.float32)
    up_float = up_all.astype(jnp.float32)
    gate_sigmoid = 1.0 / (1.0 + jnp.exp(-gate_float))
    active = (gate_float * gate_sigmoid * up_float).astype(jnp.bfloat16)
    gate_grad = (
        hidden * up_float * gate_sigmoid * (1.0 + gate_float * (1.0 - gate_sigmoid))
    ).astype(jnp.bfloat16)
    up_grad = (hidden * gate_float * gate_sigmoid).astype(jnp.bfloat16)

    partial_in = jnp.einsum(
        "nf,df->nd", gate_grad, gate_weight, preferred_element_type=jnp.float32
    ) + jnp.einsum("nf,df->nd", up_grad, up_weight, preferred_element_type=jnp.float32)
    partial_in = partial_in.reshape(Y, ZH, C, rows, feats).astype(jnp.bfloat16)
    partial_in = partial_in.swapaxes(1, 2).reshape(Y * C, ZH, rows, feats)
    partial_in = add_up(partial_in, "tensor", YC_GROUPS)
    upper = tensor // C % ZH == 1
    sent = jnp.where(upper, partial_in[0], partial_in[1])
    kept = jnp.where(upper, partial_in[1], partial_in[0])
    input_grad = (kept + lax.ppermute(sent, "tensor", ZH_SWAP)).astype(jnp.bfloat16)

    down_sum = jnp.einsum("nf,nd->fd", active, grads_all, preferred_element_type=jnp.float32)
    gate_sum = jnp.einsum("nd,nf->df", tokens_all, gate_grad, preferred_element_type=jnp.float32)
    up_sum = jnp.einsum("nd,nf->df", tokens_all, up_grad, preferred_element_type=jnp.float32)
    gate_score = jnp.abs(gate_weight.astype(jnp.float32) * gate_sum)
    up_score = jnp.abs(up_weight.astype(jnp.float32) * up_sum)
    down_score = jnp.abs(down_weight.astype(jnp.float32) * down_sum)
    return (gate_score, up_score, down_score, input_grad)


def solution(mesh):
    return jax.shard_map(
        on_device,
        mesh=mesh,
        in_specs=(
            P("tensor", "dp"),
            P("tensor", "dp"),
            P("dp", "tensor"),
            P("dp", "tensor"),
            P("dp", "tensor"),
            P("dp", "tensor"),
            P("tensor", "dp"),
        ),
        out_specs=(P("dp", "tensor"), P("dp", "tensor"), P("tensor", "dp"), P("tensor", "dp")),
        check_vma=False,
    )
```

```python
import jax
import jax.numpy as jnp
from jax import lax
from jax.sharding import PartitionSpec as P

X, ZL, Y, ZH, C = 4, 8, 4, 2, 2
X_GROUPS = [[x * ZL + z for x in range(X)] for z in range(ZL)]
Z_GROUPS = [[x * ZL + z for z in range(ZL)] for x in range(X)]
Z_BY_CORE = [
    [x * ZL + (h * C + c) * 2 + k for c in range(C) for h in range(ZH) for k in range(2)]
    for x in range(X)
]
ZH_GROUPS = [[(y * ZH + h) * C + c for h in range(ZH)] for y in range(Y) for c in range(C)]
YC_GROUPS = [[(y * ZH + h) * C + c for y in range(Y) for c in range(C)] for h in range(ZH)]
Y_GROUPS = [[(y * ZH + h) * C + c for y in range(Y)] for h in range(ZH) for c in range(C)]
C_GROUPS = [[(y * ZH + h) * C + c for c in range(C)] for y in range(Y) for h in range(ZH)]
ZH_SWAP = [(t, t ^ C) for t in range(Y * ZH * C)]
C_SWAP = [(t, t ^ 1) for t in range(Y * ZH * C)]
X_UP = [(x * ZL + z, (x + 1) % X * ZL + z) for x in range(X) for z in range(ZL)]
X_DOWN = [(x * ZL + z, (x - 1) % X * ZL + z) for x in range(X) for z in range(ZL)]


def exchange(blocks, axis, groups):
    return lax.all_to_all(blocks, axis, 0, 0, axis_index_groups=groups, tiled=True)


def gather(block, axis, groups):
    copies = jnp.broadcast_to(block[None], (len(groups[0]),) + block.shape)
    return exchange(copies, axis, groups)


def add_up(blocks, axis, groups):
    return jnp.sum(exchange(blocks, axis, groups).astype(jnp.float32), axis=0)


def pair(block, axis, perm, bit, dim):
    other = lax.ppermute(block, axis, perm)
    first = jnp.where(bit == 0, block, other)
    second = jnp.where(bit == 0, other, block)
    return jnp.stack([first, second], axis=dim)


def on_device(tokens, out_grad, gate_pre, up_pre, gate_weight, up_weight, down_weight):
    rows, feats = out_grad.shape
    toks, hid = gate_pre.shape
    n = rows * Y * ZH * C
    dp, tensor = lax.axis_index("dp"), lax.axis_index("tensor")
    x, z = dp // ZL, dp % ZL

    copies = jnp.broadcast_to(down_weight[None], (X,) + down_weight.shape)
    copies, out_grad, tokens, gate_pre, up_pre = lax.optimization_barrier(
        (copies, out_grad, tokens, gate_pre, up_pre)
    )
    down_all = exchange(copies, "dp", X_GROUPS)

    saved = jnp.stack([gate_pre, up_pre])
    saved = pair(saved, "dp", [(d, d ^ 4) for d in range(X * ZL)], z // 4, 0)

    both = jnp.stack([out_grad, tokens])
    both = lax.all_gather(both, "tensor", axis_index_groups=ZH_GROUPS, axis=1)
    saved, both = lax.optimization_barrier((saved, both))
    saved = pair(saved, "dp", [(d, d ^ 2) for d in range(X * ZL)], z // 2 % 2, 1)
    grads_y = lax.all_gather(both[0], "tensor", axis_index_groups=Y_GROUPS)
    down_all, grads_y, saved = lax.optimization_barrier((down_all, grads_y, saved))
    saved = pair(saved, "dp", [(d, d ^ 1) for d in range(X * ZL)], z % 2, 2)
    saved = saved.reshape(ZL, 2, toks, hid)

    grads_x = exchange(grads_y, "dp", X_GROUPS)
    grads_x = lax.all_gather(grads_x, "tensor", axis_index_groups=C_GROUPS)
    grads_x, saved = lax.optimization_barrier((grads_x, saved))
    partial = sum(
        jnp.einsum(
            "nd,fd->nf",
            grads_x[:, k].reshape(n // X, feats),
            down_all[k],
            preferred_element_type=jnp.float32,
        )
        for k in range(X)
    ).astype(jnp.bfloat16)

    inputs, _ = lax.optimization_barrier((both[1], partial))
    tokens_y = lax.all_gather(inputs, "tensor", axis_index_groups=Y_GROUPS)
    both = jnp.stack([grads_y, tokens_y]).reshape(2, Y * ZH, rows, feats)
    both = pair(both, "tensor", C_SWAP, tensor % C, 2)
    both = both.reshape(2, n, feats)
    grads_all, tokens_all = both[0], both[1]

    from_down = lax.ppermute(saved, "dp", X_UP)
    from_up = lax.ppermute(saved, "dp", X_DOWN)

    hidden = add_up(partial.reshape(ZL, toks, hid), "dp", Z_BY_CORE).astype(jnp.bfloat16)

    far_low = lax.ppermute(from_down[: ZL // 2], "dp", X_UP)
    far_high = lax.ppermute(from_up[ZL // 2 :], "dp", X_DOWN)

    hidden = gather(hidden, "dp", Z_GROUPS)
    hidden = gather(hidden, "dp", X_GROUPS).reshape(n, hid).astype(jnp.float32)

    full = jnp.broadcast_to(saved[None], (X,) + saved.shape)
    for block, start, half in (
        (from_down, (x + X - 1) % X, 0),
        (from_up, (x + 1) % X, 0),
        (far_low, (x + 2) % X, 0),
        (far_high, (x + 2) % X, ZL // 2),
    ):
        full = lax.dynamic_update_slice(full, block[None], (start, half, 0, 0, 0))
    gate_all = full[:, :, 0].reshape(n, hid)
    up_all = full[:, :, 1].reshape(n, hid)

    gate_float = gate_all.astype(jnp.float32)
    up_float = up_all.astype(jnp.float32)
    gate_sigmoid = 1.0 / (1.0 + jnp.exp(-gate_float))
    active = (gate_float * gate_sigmoid * up_float).astype(jnp.bfloat16)
    gate_grad = (
        hidden * up_float * gate_sigmoid * (1.0 + gate_float * (1.0 - gate_sigmoid))
    ).astype(jnp.bfloat16)
    up_grad = (hidden * gate_float * gate_sigmoid).astype(jnp.bfloat16)

    partial_in = jnp.einsum(
        "nf,df->nd", gate_grad, gate_weight, preferred_element_type=jnp.float32
    ) + jnp.einsum("nf,df->nd", up_grad, up_weight, preferred_element_type=jnp.float32)
    partial_in = partial_in.reshape(Y, ZH, C, rows, feats).astype(jnp.bfloat16)
    partial_in = partial_in.swapaxes(1, 2).reshape(Y * C, ZH, rows, feats)
    partial_in = add_up(partial_in, "tensor", YC_GROUPS)
    upper = tensor // C % ZH == 1
    sent = jnp.where(upper, partial_in[0], partial_in[1])
    kept = jnp.where(upper, partial_in[1], partial_in[0])
    input_grad = (kept + lax.ppermute(sent, "tensor", ZH_SWAP)).astype(jnp.bfloat16)

    down_sum = jnp.einsum("nf,nd->fd", active, grads_all, preferred_element_type=jnp.float32)
    gate_sum = jnp.einsum("nd,nf->df", tokens_all, gate_grad, preferred_element_type=jnp.float32)
    up_sum = jnp.einsum("nd,nf->df", tokens_all, up_grad, preferred_element_type=jnp.float32)
    gate_score = jnp.abs(gate_weight.astype(jnp.float32) * gate_sum)
    up_score = jnp.abs(up_weight.astype(jnp.float32) * up_sum)
    down_score = jnp.abs(down_weight.astype(jnp.float32) * down_sum)
    return (gate_score, up_score, down_score, input_grad)


def solution(mesh):
    return jax.shard_map(
        on_device,
        mesh=mesh,
        in_specs=(
            P("tensor", "dp"),
            P("tensor", "dp"),
            P("dp", "tensor"),
            P("dp", "tensor"),
            P("dp", "tensor"),
            P("dp", "tensor"),
            P("tensor", "dp"),
        ),
        out_specs=(P("dp", "tensor"), P("dp", "tensor"), P("tensor", "dp"), P("tensor", "dp")),
        check_vma=False,
    )
```

```python
import jax
import jax.numpy as jnp
from jax import lax
from jax.sharding import PartitionSpec as P

X, ZL, Y, ZH, C = 4, 8, 4, 2, 2
X_GROUPS = [[x * ZL + z for x in range(X)] for z in range(ZL)]
Z_GROUPS = [[x * ZL + z for z in range(ZL)] for x in range(X)]
YC_GROUPS = [[(y * ZH + h) * C + c for y in range(Y) for c in range(C)] for h in range(ZH)]
Y_GROUPS = [[(y * ZH + h) * C + c for y in range(Y)] for h in range(ZH) for c in range(C)]
C_GROUPS = [[(y * ZH + h) * C + c for c in range(C)] for y in range(Y) for h in range(ZH)]
ZH_SWAP = [(t, t ^ C) for t in range(Y * ZH * C)]
C_SWAP = [(t, t ^ 1) for t in range(Y * ZH * C)]
X_UP = [(x * ZL + z, (x + 1) % X * ZL + z) for x in range(X) for z in range(ZL)]
X_DOWN = [(x * ZL + z, (x - 1) % X * ZL + z) for x in range(X) for z in range(ZL)]


def exchange(blocks, axis, groups):
    return lax.all_to_all(blocks, axis, 0, 0, axis_index_groups=groups, tiled=True)


def gather(block, axis, groups):
    copies = jnp.broadcast_to(block[None], (len(groups[0]),) + block.shape)
    return exchange(copies, axis, groups)


def add_up(blocks, axis, groups):
    return jnp.sum(exchange(blocks, axis, groups).astype(jnp.float32), axis=0)


def pair(block, axis, perm, bit, dim):
    other = lax.ppermute(block, axis, perm)
    first = jnp.where(bit == 0, block, other)
    second = jnp.where(bit == 0, other, block)
    return jnp.stack([first, second], axis=dim)


def on_device(tokens, out_grad, gate_pre, up_pre, gate_weight, up_weight, down_weight):
    rows, feats = out_grad.shape
    toks, hid = gate_pre.shape
    n = rows * Y * ZH * C
    dp, tensor = lax.axis_index("dp"), lax.axis_index("tensor")
    x, z = dp // ZL, dp % ZL

    both = jnp.stack([out_grad, tokens])
    both = pair(both, "tensor", ZH_SWAP, tensor // C % ZH, 1)
    both = gather(both, "tensor", Y_GROUPS)

    saved = jnp.stack([gate_pre, up_pre])
    saved = pair(saved, "dp", [(d, d ^ 4) for d in range(X * ZL)], z // 4, 0)
    saved, both = lax.optimization_barrier((saved, both))
    saved = pair(saved, "dp", [(d, d ^ 2) for d in range(X * ZL)], z // 2 % 2, 1)
    saved = pair(saved, "dp", [(d, d ^ 1) for d in range(X * ZL)], z % 2, 2)
    saved = saved.reshape(ZL, 2, toks, hid)

    grads_all = lax.all_gather(both[:, 0], "tensor", axis_index_groups=C_GROUPS)
    grads_all = grads_all.transpose(1, 2, 0, 3, 4).reshape(n, feats)

    partial = jnp.einsum(
        "nd,fd->nf", grads_all, down_weight, preferred_element_type=jnp.float32
    ).astype(jnp.bfloat16)
    inputs, _ = lax.optimization_barrier((both[:, 1], partial))
    tokens_all = lax.all_gather(inputs, "tensor", axis_index_groups=C_GROUPS)
    tokens_all = tokens_all.transpose(1, 2, 0, 3, 4).reshape(n, feats)
    partial = add_up(partial.reshape(X, ZL * toks, hid), "dp", X_GROUPS).astype(jnp.bfloat16)
    partial, saved = lax.optimization_barrier((partial, saved))

    from_down = lax.ppermute(saved, "dp", X_UP)
    from_up = lax.ppermute(saved, "dp", X_DOWN)

    hidden = add_up(partial.reshape(ZL, toks, hid), "dp", Z_GROUPS).astype(jnp.bfloat16)

    far_low = lax.ppermute(from_down[: ZL // 2], "dp", X_UP)
    far_high = lax.ppermute(from_up[ZL // 2 :], "dp", X_DOWN)

    hidden = gather(hidden, "dp", Z_GROUPS)
    hidden = gather(hidden, "dp", X_GROUPS).reshape(n, hid).astype(jnp.float32)

    full = jnp.broadcast_to(saved[None], (X,) + saved.shape)
    for block, start, half in (
        (from_down, (x + X - 1) % X, 0),
        (from_up, (x + 1) % X, 0),
        (far_low, (x + 2) % X, 0),
        (far_high, (x + 2) % X, ZL // 2),
    ):
        full = lax.dynamic_update_slice(full, block[None], (start, half, 0, 0, 0))
    gate_all = full[:, :, 0].reshape(n, hid)
    up_all = full[:, :, 1].reshape(n, hid)

    gate_float = gate_all.astype(jnp.float32)
    up_float = up_all.astype(jnp.float32)
    gate_sigmoid = 1.0 / (1.0 + jnp.exp(-gate_float))
    active = (gate_float * gate_sigmoid * up_float).astype(jnp.bfloat16)
    gate_grad = (
        hidden * up_float * gate_sigmoid * (1.0 + gate_float * (1.0 - gate_sigmoid))
    ).astype(jnp.bfloat16)
    up_grad = (hidden * gate_float * gate_sigmoid).astype(jnp.bfloat16)

    partial_in = jnp.einsum(
        "nf,df->nd", gate_grad, gate_weight, preferred_element_type=jnp.float32
    ) + jnp.einsum("nf,df->nd", up_grad, up_weight, preferred_element_type=jnp.float32)
    partial_in = partial_in.reshape(Y, ZH, C, rows, feats).astype(jnp.bfloat16)
    partial_in = partial_in.swapaxes(1, 2).reshape(Y * C, ZH, rows, feats)
    partial_in = add_up(partial_in, "tensor", YC_GROUPS)
    upper = tensor // C % ZH == 1
    sent = jnp.where(upper, partial_in[0], partial_in[1])
    kept = jnp.where(upper, partial_in[1], partial_in[0])
    input_grad = (kept + lax.ppermute(sent, "tensor", ZH_SWAP)).astype(jnp.bfloat16)

    down_sum = jnp.einsum("nf,nd->fd", active, grads_all, preferred_element_type=jnp.float32)
    gate_sum = jnp.einsum("nd,nf->df", tokens_all, gate_grad, preferred_element_type=jnp.float32)
    up_sum = jnp.einsum("nd,nf->df", tokens_all, up_grad, preferred_element_type=jnp.float32)
    gate_score = jnp.abs(gate_weight.astype(jnp.float32) * gate_sum)
    up_score = jnp.abs(up_weight.astype(jnp.float32) * up_sum)
    down_score = jnp.abs(down_weight.astype(jnp.float32) * down_sum)
    return (gate_score, up_score, down_score, input_grad)


def solution(mesh):
    return jax.shard_map(
        on_device,
        mesh=mesh,
        in_specs=(
            P("tensor", "dp"),
            P("tensor", "dp"),
            P("dp", "tensor"),
            P("dp", "tensor"),
            P("dp", "tensor"),
            P("dp", "tensor"),
            P("tensor", "dp"),
        ),
        out_specs=(P("dp", "tensor"), P("dp", "tensor"), P("tensor", "dp"), P("tensor", "dp")),
        check_vma=False,
    )
```

```python
import jax
import jax.numpy as jnp
from jax import lax
from jax.sharding import PartitionSpec as P

X, ZL, Y, ZH, C = 4, 8, 4, 2, 2
X_GROUPS = [[x * ZL + z for x in range(X)] for z in range(ZL)]
Z_GROUPS = [[x * ZL + z for z in range(ZL)] for x in range(X)]
YC_GROUPS = [[(y * ZH + h) * C + c for y in range(Y) for c in range(C)] for h in range(ZH)]
Y_GROUPS = [[(y * ZH + h) * C + c for y in range(Y)] for h in range(ZH) for c in range(C)]
C_GROUPS = [[(y * ZH + h) * C + c for c in range(C)] for y in range(Y) for h in range(ZH)]
ZH_SWAP = [(t, t ^ C) for t in range(Y * ZH * C)]
C_SWAP = [(t, t ^ 1) for t in range(Y * ZH * C)]
X_UP = [(x * ZL + z, (x + 1) % X * ZL + z) for x in range(X) for z in range(ZL)]
X_DOWN = [(x * ZL + z, (x - 1) % X * ZL + z) for x in range(X) for z in range(ZL)]


def exchange(blocks, axis, groups):
    return lax.all_to_all(blocks, axis, 0, 0, axis_index_groups=groups, tiled=True)


def gather(block, axis, groups):
    copies = jnp.broadcast_to(block[None], (len(groups[0]),) + block.shape)
    return exchange(copies, axis, groups)


def add_up(blocks, axis, groups):
    return jnp.sum(exchange(blocks, axis, groups).astype(jnp.float32), axis=0)


def pair(block, axis, perm, bit, dim):
    other = lax.ppermute(block, axis, perm)
    first = jnp.where(bit == 0, block, other)
    second = jnp.where(bit == 0, other, block)
    return jnp.stack([first, second], axis=dim)


def on_device(tokens, out_grad, gate_pre, up_pre, gate_weight, up_weight, down_weight):
    rows, feats = out_grad.shape
    toks, hid = gate_pre.shape
    n = rows * Y * ZH * C
    dp, tensor = lax.axis_index("dp"), lax.axis_index("tensor")
    x, z = dp // ZL, dp % ZL

    both = jnp.stack([out_grad, tokens])
    both = pair(both, "tensor", ZH_SWAP, tensor // C % ZH, 1)
    grads_y = gather(both[0], "tensor", Y_GROUPS)

    saved = jnp.stack([gate_pre, up_pre])
    saved = pair(saved, "dp", [(d, d ^ 4) for d in range(X * ZL)], z // 4, 0)
    saved, grads_y = lax.optimization_barrier((saved, grads_y))
    saved = pair(saved, "dp", [(d, d ^ 2) for d in range(X * ZL)], z // 2 % 2, 1)
    saved = pair(saved, "dp", [(d, d ^ 1) for d in range(X * ZL)], z % 2, 2)
    saved = saved.reshape(ZL, 2, toks, hid)

    grads_all = lax.all_gather(grads_y, "tensor", axis_index_groups=C_GROUPS)
    grads_all = grads_all.transpose(1, 2, 0, 3, 4).reshape(n, feats)

    partial = jnp.einsum(
        "nd,fd->nf", grads_all, down_weight, preferred_element_type=jnp.float32
    ).astype(jnp.bfloat16)
    partial = add_up(partial.reshape(X, ZL * toks, hid), "dp", X_GROUPS).astype(jnp.bfloat16)
    partial, saved, inputs = lax.optimization_barrier((partial, saved, both[1]))

    tokens_y = lax.all_gather(inputs, "tensor", axis_index_groups=Y_GROUPS)

    from_down = lax.ppermute(saved, "dp", X_UP)
    from_up = lax.ppermute(saved, "dp", X_DOWN)

    hidden = add_up(partial.reshape(ZL, toks, hid), "dp", Z_GROUPS).astype(jnp.bfloat16)

    hidden, tokens_y = lax.optimization_barrier((hidden, tokens_y))
    tokens_all = lax.all_gather(tokens_y, "tensor", axis_index_groups=C_GROUPS)
    tokens_all = tokens_all.transpose(1, 2, 0, 3, 4).reshape(n, feats)

    far_low = lax.ppermute(from_down[: ZL // 2], "dp", X_UP)
    far_high = lax.ppermute(from_up[ZL // 2 :], "dp", X_DOWN)

    hidden = gather(hidden, "dp", Z_GROUPS)

    full = jnp.broadcast_to(saved[None], (X,) + saved.shape)
    for block, start in (
        (from_down, (x + X - 1) % X),
        (from_up, (x + 1) % X),
        (far_low, (x + 2) % X),
    ):
        full = lax.dynamic_update_slice(full, block[None], (start, 0, 0, 0, 0))
    full = lax.dynamic_update_slice(full, far_high[None], ((x + 2) % X, ZL // 2, 0, 0, 0))

    hidden = gather(hidden, "dp", X_GROUPS).reshape(n, hid).astype(jnp.float32)
    gate_all = full[:, :, 0].reshape(n, hid)
    up_all = full[:, :, 1].reshape(n, hid)

    gate_float = gate_all.astype(jnp.float32)
    up_float = up_all.astype(jnp.float32)
    gate_sigmoid = 1.0 / (1.0 + jnp.exp(-gate_float))
    active = (gate_float * gate_sigmoid * up_float).astype(jnp.bfloat16)
    gate_factor = up_float * gate_sigmoid * (1.0 + gate_float * (1.0 - gate_sigmoid))
    up_factor = gate_float * gate_sigmoid
    gate_factor, up_factor = lax.optimization_barrier((gate_factor, up_factor))
    gate_grad = (hidden * gate_factor).astype(jnp.bfloat16)
    up_grad = (hidden * up_factor).astype(jnp.bfloat16)

    partial_in = jnp.einsum(
        "nf,df->nd", gate_grad, gate_weight, preferred_element_type=jnp.float32
    ) + jnp.einsum("nf,df->nd", up_grad, up_weight, preferred_element_type=jnp.float32)
    partial_in = partial_in.reshape(Y, ZH, C, rows, feats).astype(jnp.bfloat16)
    partial_in = partial_in.swapaxes(1, 2).reshape(Y * C, ZH, rows, feats)
    partial_in = add_up(partial_in, "tensor", YC_GROUPS)
    upper = tensor // C % ZH == 1
    sent = jnp.where(upper, partial_in[0], partial_in[1])
    kept = jnp.where(upper, partial_in[1], partial_in[0])
    input_grad = (kept + lax.ppermute(sent, "tensor", ZH_SWAP)).astype(jnp.bfloat16)

    down_sum = jnp.einsum("nf,nd->fd", active, grads_all, preferred_element_type=jnp.float32)
    gate_sum = jnp.einsum("nd,nf->df", tokens_all, gate_grad, preferred_element_type=jnp.float32)
    up_sum = jnp.einsum("nd,nf->df", tokens_all, up_grad, preferred_element_type=jnp.float32)
    gate_score = jnp.abs(gate_weight.astype(jnp.float32) * gate_sum)
    up_score = jnp.abs(up_weight.astype(jnp.float32) * up_sum)
    down_score = jnp.abs(down_weight.astype(jnp.float32) * down_sum)
    return (gate_score, up_score, down_score, input_grad)


def solution(mesh):
    return jax.shard_map(
        on_device,
        mesh=mesh,
        in_specs=(
            P("tensor", "dp"),
            P("tensor", "dp"),
            P("dp", "tensor"),
            P("dp", "tensor"),
            P("dp", "tensor"),
            P("dp", "tensor"),
            P("tensor", "dp"),
        ),
        out_specs=(P("dp", "tensor"), P("dp", "tensor"), P("tensor", "dp"), P("tensor", "dp")),
        check_vma=False,
    )
```

```python
import jax
import jax.numpy as jnp
from jax import lax
from jax.sharding import PartitionSpec as P

X, ZL, Y, ZH, C = 4, 8, 4, 2, 2
X_GROUPS = [[x * ZL + z for x in range(X)] for z in range(ZL)]
Z_GROUPS = [[x * ZL + z for z in range(ZL)] for x in range(X)]
YC_GROUPS = [[(y * ZH + h) * C + c for y in range(Y) for c in range(C)] for h in range(ZH)]
Y_GROUPS = [[(y * ZH + h) * C + c for y in range(Y)] for h in range(ZH) for c in range(C)]
C_GROUPS = [[(y * ZH + h) * C + c for c in range(C)] for y in range(Y) for h in range(ZH)]
ZH_SWAP = [(t, t ^ C) for t in range(Y * ZH * C)]
C_SWAP = [(t, t ^ 1) for t in range(Y * ZH * C)]
X_UP = [(x * ZL + z, (x + 1) % X * ZL + z) for x in range(X) for z in range(ZL)]
X_DOWN = [(x * ZL + z, (x - 1) % X * ZL + z) for x in range(X) for z in range(ZL)]


def exchange(blocks, axis, groups):
    return lax.all_to_all(blocks, axis, 0, 0, axis_index_groups=groups, tiled=True)


def gather(block, axis, groups):
    copies = jnp.broadcast_to(block[None], (len(groups[0]),) + block.shape)
    return exchange(copies, axis, groups)


def add_up(blocks, axis, groups):
    return jnp.sum(exchange(blocks, axis, groups).astype(jnp.float32), axis=0)


def pair(block, axis, perm, bit, dim):
    other = lax.ppermute(block, axis, perm)
    first = jnp.where(bit == 0, block, other)
    second = jnp.where(bit == 0, other, block)
    return jnp.stack([first, second], axis=dim)


def on_device(tokens, out_grad, gate_pre, up_pre, gate_weight, up_weight, down_weight):
    rows, feats = out_grad.shape
    toks, hid = gate_pre.shape
    n = rows * Y * ZH * C
    dp, tensor = lax.axis_index("dp"), lax.axis_index("tensor")
    x, z = dp // ZL, dp % ZL

    both = jnp.stack([out_grad, tokens])
    both = pair(both, "tensor", ZH_SWAP, tensor // C % ZH, 1)
    grads_y = gather(both[0], "tensor", Y_GROUPS)

    saved = jnp.stack([gate_pre, up_pre])
    saved = pair(saved, "dp", [(d, d ^ 4) for d in range(X * ZL)], z // 4, 0)
    saved, _ = lax.optimization_barrier((saved, grads_y))
    saved = pair(saved, "dp", [(d, d ^ 2) for d in range(X * ZL)], z // 2 % 2, 1)
    saved = pair(saved, "dp", [(d, d ^ 1) for d in range(X * ZL)], z % 2, 2)
    saved = saved.reshape(ZL, 2, toks, hid)

    grads_all = lax.all_gather(grads_y, "tensor", axis_index_groups=C_GROUPS)
    grads_all = grads_all.transpose(1, 2, 0, 3, 4).reshape(n, feats)

    partial = jnp.einsum(
        "nd,fd->nf", grads_all, down_weight, preferred_element_type=jnp.float32
    ).astype(jnp.bfloat16)
    partial = add_up(partial.reshape(X, ZL * toks, hid), "dp", X_GROUPS).astype(jnp.bfloat16)
    partial, saved, inputs = lax.optimization_barrier((partial, saved, both[1]))

    tokens_y = lax.all_gather(inputs, "tensor", axis_index_groups=Y_GROUPS)

    from_down = lax.ppermute(saved, "dp", X_UP)
    from_up = lax.ppermute(saved, "dp", X_DOWN)

    hidden = add_up(partial.reshape(ZL, toks, hid), "dp", Z_GROUPS).astype(jnp.bfloat16)

    hidden, tokens_y = lax.optimization_barrier((hidden, tokens_y))
    tokens_all = lax.all_gather(tokens_y, "tensor", axis_index_groups=C_GROUPS)
    tokens_all = tokens_all.transpose(1, 2, 0, 3, 4).reshape(n, feats)

    far_low = lax.ppermute(from_down[: ZL // 2], "dp", X_UP)
    far_high = lax.ppermute(from_up[ZL // 2 :], "dp", X_DOWN)

    hidden = gather(hidden, "dp", Z_GROUPS)

    full = jnp.broadcast_to(saved[None], (X,) + saved.shape)
    for block, start in (
        (from_down, (x + X - 1) % X),
        (from_up, (x + 1) % X),
        (far_low, (x + 2) % X),
    ):
        full = lax.dynamic_update_slice(full, block[None], (start, 0, 0, 0, 0))
    full = lax.dynamic_update_slice(full, far_high[None], ((x + 2) % X, ZL // 2, 0, 0, 0))

    hidden = gather(hidden, "dp", X_GROUPS).reshape(n, hid).astype(jnp.float32)
    gate_all = full[:, :, 0].reshape(n, hid)
    up_all = full[:, :, 1].reshape(n, hid)

    gate_float = gate_all.astype(jnp.float32)
    up_float = up_all.astype(jnp.float32)
    gate_sigmoid = 1.0 / (1.0 + jnp.exp(-gate_float))
    active = (gate_float * gate_sigmoid * up_float).astype(jnp.bfloat16)
    gate_factor = up_float * gate_sigmoid * (1.0 + gate_float * (1.0 - gate_sigmoid))
    up_factor = gate_float * gate_sigmoid
    gate_grad = (hidden * gate_factor).astype(jnp.bfloat16)
    up_grad = (hidden * up_factor).astype(jnp.bfloat16)

    partial_in = jnp.einsum(
        "nf,df->nd", gate_grad, gate_weight, preferred_element_type=jnp.float32
    ) + jnp.einsum("nf,df->nd", up_grad, up_weight, preferred_element_type=jnp.float32)
    partial_in = partial_in.reshape(Y, ZH, C, rows, feats).astype(jnp.bfloat16)
    partial_in = partial_in.swapaxes(1, 2).reshape(Y * C, ZH, rows, feats)
    partial_in = add_up(partial_in, "tensor", YC_GROUPS)
    upper = tensor // C % ZH == 1
    sent = jnp.where(upper, partial_in[0], partial_in[1])
    kept = jnp.where(upper, partial_in[1], partial_in[0])
    input_grad = (kept + lax.ppermute(sent, "tensor", ZH_SWAP)).astype(jnp.bfloat16)

    down_sum = jnp.einsum("nf,nd->fd", active, grads_all, preferred_element_type=jnp.float32)
    gate_sum = jnp.einsum("nd,nf->df", tokens_all, gate_grad, preferred_element_type=jnp.float32)
    up_sum = jnp.einsum("nd,nf->df", tokens_all, up_grad, preferred_element_type=jnp.float32)
    gate_score = jnp.abs(gate_weight.astype(jnp.float32) * gate_sum)
    up_score = jnp.abs(up_weight.astype(jnp.float32) * up_sum)
    down_score = jnp.abs(down_weight.astype(jnp.float32) * down_sum)
    return (gate_score, up_score, down_score, input_grad)


def solution(mesh):
    return jax.shard_map(
        on_device,
        mesh=mesh,
        in_specs=(
            P("tensor", "dp"),
            P("tensor", "dp"),
            P("dp", "tensor"),
            P("dp", "tensor"),
            P("dp", "tensor"),
            P("dp", "tensor"),
            P("tensor", "dp"),
        ),
        out_specs=(P("dp", "tensor"), P("dp", "tensor"), P("tensor", "dp"), P("tensor", "dp")),
        check_vma=False,
    )
```
